128 devices in a mesh: region: 4 (over y), member: 32 (over z, x, core).
Axes of the slice: x: 4, y: 4, z: 4, core: 2. Of those that a mesh axis runs over, the one named last changes fastest.
Arguments:
- member_perts: bfloat16 [256, 2, 1024, 512], P('member', None, 'region'), may hold values from -6 to 6
- alpha: float32 [256, 1024, 512], P('member', 'region'), may hold values from -0.6 to 0.6
- background: float32 [2, 1024, 512], P(None, ('region', 'member')), may hold values from -6 to 6
- obs_value: float32 [128, 112, 256], P(('region', 'member')), may hold values from -6 to 6
- obs_weight: float32 [128, 112, 256], P(('region', 'member')), may hold values from 0.5 to 8
- observed_subtile_entry: int32 [128, 112, 256], P(('region', 'member')), may hold values from 0 to 8191
- block_owner: int32 [128, 112, 1], P(('region', 'member')), may hold values from 0 to 127; in each aligned block of 112 rows (0 to 111, 112 to 223, ..., all dimensions but the last counted through in order) at most 2 rows name the same one
- block_count: int32 [128, 112], P(('region', 'member')), may hold values from 1 to 256, 25088 in all within a row
Outputs:
- gradient: float32 [256, 1024, 512], P('member', 'region')
The draws below stay inside these ranges and needn't reach their ends.
Inputs may be any that keep to these rules, and one draw needn't show every extreme that they name: `block_owner`: no device holds more than 2 blocks of one tile owner. `block_count`: the counts of one device sum to 25088. `observed_subtile_entry`: an index into the owner's sub-tile flattened over fields, rows and columns.
All inputs are finite; a program needn't handle non-finite values.
Results may differ from the reference program's by a relative error of at most 0.0003.
Values sent between devices are 32-bit elements; how exact they have to be, the bound alone decides.
No kernel may reach another device: no remote copies, remote signals or barrier semaphores. Data moves between devices by JAX's collectives and lax.ppermute only.
A program may use at most 128 MiB of HBM per device.

```python
import math
import jax
import jax.numpy as jnp
import numpy as np
from jax import lax

FIELD_TOTAL = 2
GRID_COLUMNS = 512
BLOCK_SLOTS = 256
CAP = 2
HALF = 31
ENS = 256
NY = 1024
OWNER_GRID_ROWS = 8
BLOCKS_PER_UNIT = 112
N_REGION = 4
N_MEMBER = 32


def with_ends(drawn, rng, least, largest):
    extent = drawn.shape
    index_at = [jax.random.randint(jax.random.fold_in(rng, axis), (), 0, extent[axis]) for axis in range(len(extent))]
    drawn = drawn.at[tuple(index_at)].set(least)
    longest = extent.index(max(extent))
    index_at[longest] = (index_at[longest] + 1) % extent[longest]
    return drawn.at[tuple(index_at)].set(largest)


def with_spikes(result, rng, source, target, blocks, factor):
    def block_of(axis_at):
        return (jnp.arange(result.shape[axis_at]) // (result.shape[axis_at] // blocks)).reshape((-1,) + (1,) * (result.ndim - 1 - axis_at))

    one_side = jax.random.permutation(rng, blocks)[block_of(target)]
    other_side = (block_of(target) + blocks // 2) % blocks
    return jnp.where((block_of(source) == one_side) | (block_of(source) == other_side), factor * result, result)


def steps_of(rng, extent, cuts, least, largest):
    factor_of, own = 1.0, jax.random.fold_in(rng, 6)
    for position, shards_of in cuts:
        heights = jnp.exp(jax.random.uniform(jax.random.fold_in(own, position), (shards_of,), jnp.float32, least / len(cuts), largest / len(cuts)))
        factor_of = factor_of * jnp.repeat(heights, extent[position] // shards_of).reshape([-1 if axis == position else 1 for axis in range(len(extent))])
    return factor_of


def length_profile(number_of, total, limit, lean):
    loads = [(1 << 20) // math.isqrt(rank ** lean) + 1 for rank in range(2, number_of + 1)]
    spare, holding = total - limit - (number_of - 1), [1] * (number_of - 1)
    while spare > 0:
        free = [i for i in range(number_of - 1) if holding[i] < limit]
        pool, left = sum([loads[i] for i in free]), spare
        for i in free:
            addition = min(limit - holding[i], max(1, left * loads[i] // pool), spare)
            holding[i] = holding[i] + addition
            spare = spare - addition
    return np.array([limit] + holding)


def uneven(rng, amount, total, bound, skew):
    if amount == 2:
        one = jax.random.randint(rng, (), max(1, total - bound), min(bound, total - 1) + 1)
        return jnp.stack([one, total - one])
    tallies = jnp.asarray(length_profile(amount, total, bound, skew), jnp.int32)
    pairs = (amount - 1) // 2
    source_of, taker = tallies[1:1 + 2 * pairs:2], tallies[2:2 + 2 * pairs:2]
    room = jnp.minimum(source_of - 1, bound - taker)
    shifted = jax.random.randint(jax.random.fold_in(rng, 1), (pairs,), 0, 1 << 20) % (room + 1)
    tallies = tallies.at[1:1 + 2 * pairs:2].set(source_of - shifted).at[2:2 + 2 * pairs:2].set(taker + shifted)
    return tallies[jax.random.permutation(jax.random.fold_in(rng, 2), amount)]


def deal_out(rng, own, number, rows, count, top, reach, skew):
    ranking = jax.random.permutation(rng, count)
    heavy_load, ordinary = shares(count, rows * top, reach, skew, True), shares(count, rows * top, reach, skew, False)
    places = jnp.arange(count)

    def named(lengths, offset_by):
        used = int((lengths > 0).sum())
        fixed = max(1, used // 4)
        shifted = fixed + (places - fixed + offset_by * (used - fixed)) % max(1, count - fixed)
        return jnp.zeros((count,), jnp.int32).at[ranking[jnp.where(places < fixed, places, shifted)]].set(jnp.asarray(lengths, jnp.int32))

    lengths = jnp.where(number % 4 == 0, named(heavy_load, number // 4), named(ordinary, number - number // 4 - 1))
    mixed = jax.random.permutation(jax.random.fold_in(own, 3), count)
    source_of, sink = mixed[0:count // 2 * 2:2], mixed[1:count // 2 * 2:2]
    room = jnp.minimum(lengths[source_of] - 1, reach - lengths[sink]) // 2
    room = jnp.where((source_of == ranking[0]) | (sink == ranking[0]) | (lengths[sink] == 0), 0, jnp.maximum(room, 0))
    shifted = jax.random.randint(jax.random.fold_in(own, 4), (count // 2,), 0, 1 << 20) % (room + 1)
    lengths = lengths.at[source_of].add(-shifted).at[sink].add(shifted)
    labels = jnp.searchsorted(jnp.cumsum(lengths), jnp.arange(rows * top), side="right").astype(jnp.int32)
    grid = labels.reshape(top, rows).T
    grid = grid[jax.random.permutation(jax.random.fold_in(own, 1), rows)]
    offset_by = jax.random.randint(jax.random.fold_in(own, 2), (rows, 1), 0, top)
    return jnp.take_along_axis(grid, (jnp.arange(top)[None, :] + offset_by) % top, axis=1)


def shares(amount, total, limit, slope, full):
    weights = [(1 << 20) // math.isqrt(standing ** slope) + 1 for standing in range(1, amount + 1)]
    largest = limit if full else min(limit, max(-(-total // amount), total * weights[0] // sum(weights)))
    least = 1 if total - largest >= amount - 1 else 0
    holding, rest = [largest] + [least] * (amount - 1), total - largest - least * (amount - 1)
    while rest > 0:
        movable = [i for i in range(1, amount) if holding[i] < largest] or [i for i in range(1, amount) if holding[i] < limit]
        whole, left = sum([weights[i] for i in movable]), rest
        for i in movable:
            more = min(limit - holding[i], max(1, left * weights[i] // whole), rest)
            holding[i] = holding[i] + more
            rest = rest - more
    return np.array(holding)


def gaussian(key, shape, deviation, bound, pieces=(), kind=jnp.bfloat16):
    factor_of = steps_of(key, shape, pieces, -0.22, 0.18) if pieces else 1.0
    array = jax.random.normal(key, shape, jnp.float32) * deviation * factor_of
    return jnp.minimum(jnp.maximum(array, -bound), bound).astype(kind)


def gaussian_with(own_key, shape, deviation, limit, pieces, heavy, kind=jnp.bfloat16):
    array = deviation * jax.random.normal(own_key, shape, jnp.float32)
    if pieces:
        array = array * steps_of(own_key, shape, pieces, -0.22, 0.18)
    return jnp.clip(with_spikes(array, jax.random.fold_in(own_key, 3), *heavy), -limit, limit).astype(kind)


def setup_inputs(seed: int = 0) -> dict:
    key_of = jax.random.split(jax.random.key(seed), 9)
    member_perts = gaussian_with(key_of[0], (ENS, FIELD_TOTAL, NY, GRID_COLUMNS), 1.0, 6.0, ((0, 32), (2, 4)), (0, 2, 32, 2.75))
    alpha = gaussian(key_of[1], (ENS, NY, GRID_COLUMNS), 0.1, 0.6, ((0, 32), (1, 4)), jnp.float32)
    background = gaussian(key_of[2], (FIELD_TOTAL, NY, GRID_COLUMNS), 1.0, 6.0, ((1, 128),), jnp.float32)
    obs_value = gaussian(key_of[3], (N_REGION * N_MEMBER, BLOCKS_PER_UNIT, BLOCK_SLOTS), 1.0, 6.0, ((0, 128),), jnp.float32)
    obs_weight = jnp.clip(jnp.exp(math.log(8.0) - 2.7725887 * jax.random.uniform(key_of[4], (N_REGION * N_MEMBER, BLOCKS_PER_UNIT, BLOCK_SLOTS), jnp.float32) ** steps_of(key_of[4], (N_REGION * N_MEMBER, BLOCKS_PER_UNIT, BLOCK_SLOTS), ((0, 128),), -0.2, 0.2)), 0.5, 8.0)
    observed_subtile_entry = with_ends(jax.random.randint(key_of[5], (N_REGION * N_MEMBER, BLOCKS_PER_UNIT, BLOCK_SLOTS), 0, FIELD_TOTAL * OWNER_GRID_ROWS * GRID_COLUMNS), jax.random.fold_in(key_of[5], 1), 0, (FIELD_TOTAL * OWNER_GRID_ROWS * GRID_COLUMNS) - 1).astype(jnp.int32)
    block_owner_keys = jax.random.split(jax.random.fold_in(key_of[6], 1), (N_REGION * N_MEMBER) * BLOCKS_PER_UNIT // BLOCKS_PER_UNIT)
    block_owner_turns = jax.random.permutation(jax.random.fold_in(key_of[6], 3), (N_REGION * N_MEMBER) * BLOCKS_PER_UNIT // BLOCKS_PER_UNIT)
    block_owner = jax.vmap(lambda own, number: deal_out(jax.random.fold_in(key_of[6], 2), own, number, BLOCKS_PER_UNIT, N_REGION * N_MEMBER, 1, CAP, 2))(block_owner_keys, block_owner_turns).reshape((N_REGION * N_MEMBER, BLOCKS_PER_UNIT, 1))
    block_count = jax.vmap(lambda own: uneven(own, BLOCKS_PER_UNIT, BLOCKS_PER_UNIT * BLOCK_SLOTS * 7 // 8, BLOCK_SLOTS, 1))(jax.random.split(key_of[7], (N_REGION * N_MEMBER))).reshape((N_REGION * N_MEMBER, BLOCKS_PER_UNIT)).astype(jnp.int32)
    return dict(member_perts=member_perts, alpha=alpha, background=background, obs_value=obs_value, obs_weight=obs_weight, observed_subtile_entry=observed_subtile_entry, block_owner=block_owner, block_count=block_count)


length_scale = 16.0

def kernel_taps():
    offsets = jnp.arange(-HALF, HALF + 1).astype(jnp.float32)
    raw = jnp.exp(-offsets * offsets / (2.0 * length_scale * length_scale))
    return raw / jnp.sqrt(jnp.sum(raw * raw))

def localize(fields):
    kernel = kernel_taps().astype(fields.dtype)
    stacked = fields[:, None]
    vertical = lax.conv_general_dilated(stacked, kernel.reshape(1, 1, -1, 1), (1, 1), ((HALF, HALF), (0, 0)), precision=lax.Precision.HIGHEST)
    across = lax.conv_general_dilated(vertical, kernel.reshape(1, 1, 1, -1), (1, 1), ((0, 0), (HALF, HALF)), precision=lax.Precision.HIGHEST)
    return across[:, 0]

def reference(member_perts, alpha, background, obs_value, obs_weight, observed_subtile_entry, block_owner, block_count):
    ens_scale = 1.0 / jnp.sqrt(jnp.float32(ENS - 1))
    group_size = math.gcd(ENS, 16)
    group_count = ENS // group_size
    perts_grouped = member_perts.reshape(group_count, group_size, FIELD_TOTAL, NY, GRID_COLUMNS)
    alpha_grouped = alpha.reshape(group_count, group_size, NY, GRID_COLUMNS)

    def add_group(running, inputs):
        member_block, coeffs = inputs
        spread = localize(coeffs)
        return (running + lax.optimization_barrier(jnp.sum(member_block.astype(jnp.float32) * spread[:, None], axis=0)), None)
    running, unused = lax.scan(add_group, jnp.zeros((FIELD_TOTAL, NY, GRID_COLUMNS), jnp.float32), (perts_grouped, alpha_grouped))
    state = background + ens_scale * running
    owning_unit = jnp.broadcast_to(block_owner, observed_subtile_entry.shape)
    slot_pos = jnp.arange(BLOCK_SLOTS)[None, None, :]
    live_slot = slot_pos < block_count[:, :, None]
    subtile_size = OWNER_GRID_ROWS * GRID_COLUMNS
    field_index = observed_subtile_entry // subtile_size
    leftover_count = observed_subtile_entry % subtile_size
    subtile_row_index = owning_unit * OWNER_GRID_ROWS + leftover_count // GRID_COLUMNS
    column = leftover_count % GRID_COLUMNS
    flat_index = ((field_index * NY + subtile_row_index) * GRID_COLUMNS + column).reshape(-1)
    picked = state.reshape(-1)[flat_index].reshape(observed_subtile_entry.shape)
    misfit = jnp.where(live_slot, obs_weight * (picked - obs_value), 0.0)
    adjoint = jnp.zeros((FIELD_TOTAL * NY * GRID_COLUMNS,), jnp.float32).at[flat_index].add(misfit.reshape(-1)).reshape(FIELD_TOTAL, NY, GRID_COLUMNS)

    def group_gradient(inputs):
        member_block, coeffs = inputs
        product = lax.optimization_barrier(jnp.sum(member_block.astype(jnp.float32) * adjoint[None], axis=1))
        return coeffs + ens_scale * localize(product)
    gradient = lax.map(group_gradient, (perts_grouped, alpha_grouped))
    return gradient.reshape(ENS, NY, GRID_COLUMNS)
```

```python
import math

import jax
import jax.numpy as jnp
import ml_dtypes
import numpy as np
from jax import lax
from jax.experimental import pallas as pl
from jax.experimental.pallas import tpu as pltpu
from jax.sharding import PartitionSpec as P

HALF = 31
LENGTH_SCALE = 16.0
MEMBERS = 8
ROWS = 256
COLS = 512
EDGE = 32
SUB = 8
ENS_SCALE = 1.0 / math.sqrt(255.0)
F32 = jnp.float32
BF16 = jnp.bfloat16
PARAMS = pltpu.CompilerParams(vmem_limit_bytes=40 * 1024 * 1024)


def taps(offset):
    whole = np.arange(-HALF, HALF + 1).astype(np.float64)
    raw = np.exp(-whole * whole / (2.0 * LENGTH_SCALE**2))
    kernel = np.exp(-(offset.astype(np.float64) ** 2) / (2.0 * LENGTH_SCALE**2))
    return np.where(np.abs(offset) <= HALF, kernel / np.sqrt(np.sum(raw * raw)), 0.0)


def split_const(matrix):
    high = matrix.astype(ml_dtypes.bfloat16)
    low = (matrix - high.astype(np.float64)).astype(ml_dtypes.bfloat16)
    return np.stack([high, low])


def band(size):
    index = np.arange(size)
    return split_const(taps(index[None, :] - index[:, None]))


def edge_bands():
    index = np.arange(EDGE)
    top = taps(index[None, :] - EDGE - index[:, None])
    bottom = taps(index[None, :] + EDGE - index[:, None])
    eye = np.eye(MEMBERS)
    return (split_const(np.kron(eye, top)), split_const(np.kron(eye, bottom)))


def split(value):
    high = value.astype(BF16)
    return high, (value - high.astype(F32)).astype(BF16)


def mm(a, b):
    return jnp.dot(a, b, preferred_element_type=F32)


def conv(value, down_ref, across_ref):
    high, low = split(value)
    rows = mm(down_ref[0], high) + mm(down_ref[0], low) + mm(down_ref[1], high)
    high, low = split(rows)
    parts = []
    for block in range(2):
        k = slice(128 * block, 128 * block + 384)
        n = slice(256 * block, 256 * block + 256)
        parts.append(
            mm(high[:, k], across_ref[0, k, n])
            + mm(low[:, k], across_ref[0, k, n])
            + mm(high[:, k], across_ref[1, k, n])
        )
    return jnp.concatenate(parts, axis=1)


def whole(shape):
    return pl.BlockSpec(shape, lambda *_: (0,) * len(shape))


def cost(flops, nbytes):
    return pl.CostEstimate(flops=flops, bytes_accessed=nbytes, transcendentals=0)


def forward_body(alpha_ref, perts_ref, down_ref, across_ref, term_ref):
    spread = conv(alpha_ref[0], down_ref, across_ref)
    step = pl.program_id(0)
    for field in range(2):
        add = perts_ref[0, field].astype(F32) * spread

        @pl.when(step == 0)
        def _():
            term_ref[field] = add

        @pl.when(step > 0)
        def _():
            term_ref[field] += add


def forward(alpha, perts, down, across):
    return pl.pallas_call(
        forward_body,
        grid=(MEMBERS,),
        in_specs=[
            pl.BlockSpec((1, ROWS, COLS), lambda k: (k, 0, 0)),
            pl.BlockSpec((1, 2, ROWS, COLS), lambda k: (k, 0, 0, 0)),
            whole((2, ROWS, ROWS)),
            whole((2, COLS, COLS)),
        ],
        out_specs=whole((2, ROWS, COLS)),
        out_shape=jax.ShapeDtypeStruct((2, ROWS, COLS), F32),
        compiler_params=PARAMS,
        cost_estimate=cost(4 * 10**9, 10 * 2**20),
        name="forward_own",
    )(alpha, perts, down, across)


def forward_edge_body(
    term_ref, top_ref, bottom_ref, pt_ref, pb_ref, vt_ref, vb_ref, across_ref, mine_ref, other_ref, scr
):
    core = lax.rem(lax.axis_index("member"), 2)
    for field in range(2):
        scr[field] = term_ref[field].reshape(16, 2, SUB, COLS)
    for halo_ref, p_ref, v_ref, base in (
        (top_ref, pt_ref, vt_ref, 0),
        (bottom_ref, pb_ref, vb_ref, 14),
    ):
        spread = conv(halo_ref[...].reshape(MEMBERS * EDGE, COLS), v_ref, across_ref)
        spread = spread.reshape(MEMBERS, EDGE, COLS)
        for field in range(2):
            add = jnp.sum(p_ref[:, field].astype(F32) * spread, axis=0)
            scr[field, base : base + 2] += add.reshape(2, 2, SUB, COLS)
    for field in range(2):
        mine_ref[:, field] = scr[field, :, core]
        other_ref[:, field] = scr[field, :, 1 - core]


def forward_edge(term, top, bottom, perts, vt, vb, across):
    piece = jax.ShapeDtypeStruct((16, 2, SUB, COLS), F32)
    return pl.pallas_call(
        forward_edge_body,
        grid=(1,),
        in_specs=[
            whole((2, ROWS, COLS)),
            whole((MEMBERS, EDGE, COLS)),
            whole((MEMBERS, EDGE, COLS)),
            pl.BlockSpec((MEMBERS, 2, EDGE, COLS), lambda i: (0, 0, 0, 0)),
            pl.BlockSpec((MEMBERS, 2, EDGE, COLS), lambda i: (0, 0, ROWS // EDGE - 1, 0)),
            whole((2, 256, 256)),
            whole((2, 256, 256)),
            whole((2, COLS, COLS)),
        ],
        out_specs=[whole((16, 2, SUB, COLS))] * 2,
        out_shape=[piece, piece],
        scratch_shapes=[pltpu.VMEM((2, 16, 2, SUB, COLS), F32)],
        compiler_params=PARAMS,
        cost_estimate=cost(10**9, 6 * 2**20),
        name="forward_edge",
    )(term, top, bottom, perts, perts, vt, vb, across)


def stage_z_body(mine_ref, got_ref, *outs):
    z = lax.axis_index("member") // 8
    for step in range(4):
        at = pl.ds(lax.rem(z + step, 4) * 4, 4)
        outs[step][...] = mine_ref[at] + got_ref[at]


def stage_z(mine, got):
    piece = jax.ShapeDtypeStruct((4, 2, SUB, COLS), F32)
    return pl.pallas_call(
        stage_z_body, out_shape=[piece] * 4, compiler_params=PARAMS,
        cost_estimate=cost(10**6, 2**20), name="stage_z",
    )(mine, got)


def stage_x_body(keep_ref, a_ref, b_ref, c_ref, *outs):
    x = lax.rem(lax.axis_index("member") // 2, 4)
    for step in range(4):
        at = lax.rem(x + step, 4)
        outs[step][...] = (keep_ref[at] + a_ref[at]) + (b_ref[at] + c_ref[at])


def stage_x(keep, got):
    piece = jax.ShapeDtypeStruct((2, SUB, COLS), F32)
    return pl.pallas_call(
        stage_x_body, out_shape=[piece] * 4, compiler_params=PARAMS,
        cost_estimate=cost(10**6, 2**20), name="stage_x",
    )(keep, *got)


def adjoint_body(back_ref, keep_ref, a_ref, b_ref, c_ref, w_ref, v_ref, out_ref):
    total = (keep_ref[...] + a_ref[...]) + (b_ref[...] + c_ref[...])
    state = back_ref[...] + ENS_SCALE * total
    out_ref[...] = state * w_ref[...] - v_ref[...]


def adjoint_of(back, keep, got, w, v):
    return pl.pallas_call(
        adjoint_body, out_shape=jax.ShapeDtypeStruct((2, SUB, COLS), F32),
        compiler_params=PARAMS, cost_estimate=cost(10**5, 2**18), name="adjoint",
    )(back, keep, *got, w, v)


def gather_x_body(own_ref, a_ref, b_ref, c_ref, out_ref):
    x = lax.rem(lax.axis_index("member") // 2, 4)
    for step, ref in enumerate((own_ref, a_ref, b_ref, c_ref)):
        out_ref[lax.rem(x + 4 - step, 4)] = ref[...]


def gather_x(own, got):
    return pl.pallas_call(
        gather_x_body, out_shape=jax.ShapeDtypeStruct((4, 2, SUB, COLS), F32),
        compiler_params=PARAMS, cost_estimate=cost(10**5, 2**18), name="gather_x",
    )(own, *got)


def product_edge_body(*refs):
    mine, other = refs[0:4], refs[4:8]
    pt_ref, pb_ref, adj_ref, top_ref, bottom_ref = refs[8:]
    me = lax.axis_index("member")
    z = me // 8
    core = lax.rem(me, 2)
    for step in range(4):
        at = lax.rem(z + 4 - step, 4)
        for x in range(4):
            adj_ref[:, at, x, core] = mine[step][x]
            adj_ref[:, at, x, 1 - core] = other[step][x]
    for p_ref, out_ref, z_at, x_at in ((pt_ref, top_ref, 0, 0), (pb_ref, bottom_ref, 3, 2)):
        first = adj_ref[0, z_at, x_at : x_at + 2].reshape(EDGE, COLS)
        second = adj_ref[1, z_at, x_at : x_at + 2].reshape(EDGE, COLS)
        for k in range(MEMBERS):
            out_ref[k] = p_ref[k, 0].astype(F32) * first + p_ref[k, 1].astype(F32) * second


def product_edge(mine, other, perts):
    edge = jax.ShapeDtypeStruct((MEMBERS, EDGE, COLS), F32)
    full = (2, 4, 4, 2, SUB, COLS)
    return pl.pallas_call(
        product_edge_body,
        grid=(1,),
        in_specs=[whole((4, 2, SUB, COLS))] * 8
        + [
            pl.BlockSpec((MEMBERS, 2, EDGE, COLS), lambda i: (0, 0, 0, 0)),
            pl.BlockSpec((MEMBERS, 2, EDGE, COLS), lambda i: (0, 0, ROWS // EDGE - 1, 0)),
        ],
        out_specs=[whole(full), whole((MEMBERS, EDGE, COLS)), whole((MEMBERS, EDGE, COLS))],
        out_shape=[jax.ShapeDtypeStruct(full, F32), edge, edge],
        compiler_params=PARAMS,
        cost_estimate=cost(10**6, 4 * 2**20),
        name="product_edge",
    )(*mine, *other, perts, perts)


def backward_body(alpha_ref, perts_ref, adj_ref, down_ref, across_ref, out_ref):
    product = perts_ref[0, 0].astype(F32) * adj_ref[0] + perts_ref[0, 1].astype(F32) * adj_ref[1]
    out_ref[0] = alpha_ref[0] + ENS_SCALE * conv(product, down_ref, across_ref)


def backward(alpha, perts, adj, down, across):
    return pl.pallas_call(
        backward_body,
        grid=(MEMBERS,),
        in_specs=[
            pl.BlockSpec((1, ROWS, COLS), lambda k: (k, 0, 0)),
            pl.BlockSpec((1, 2, ROWS, COLS), lambda k: (k, 0, 0, 0)),
            whole((2, ROWS, COLS)),
            whole((2, ROWS, ROWS)),
            whole((2, COLS, COLS)),
        ],
        out_specs=pl.BlockSpec((1, ROWS, COLS), lambda k: (k, 0, 0)),
        out_shape=jax.ShapeDtypeStruct((MEMBERS, ROWS, COLS), F32),
        compiler_params=PARAMS,
        cost_estimate=cost(4 * 10**9, 14 * 2**20),
        name="backward_own",
    )(alpha, perts, adj, down, across)


def backward_edge_body(grad_ref, top_ref, bottom_ref, v_ref, across_ref, out_ref):
    def add(halo_ref):
        spread = conv(halo_ref[...].reshape(MEMBERS * EDGE, COLS), v_ref.at[0], across_ref)
        out_ref[...] = grad_ref[...] + ENS_SCALE * spread.reshape(MEMBERS, EDGE, COLS)

    @pl.when(pl.program_id(0) == 0)
    def _():
        add(top_ref)

    @pl.when(pl.program_id(0) == 1)
    def _():
        add(bottom_ref)


def backward_edge(grad, top, bottom, edges, across):
    block = pl.BlockSpec((MEMBERS, EDGE, COLS), lambda i: (0, i * (ROWS // EDGE - 1), 0))
    return pl.pallas_call(
        backward_edge_body,
        grid=(2,),
        in_specs=[
            block,
            whole((MEMBERS, EDGE, COLS)),
            whole((MEMBERS, EDGE, COLS)),
            pl.BlockSpec((1, 2, 256, 256), lambda i: (i, 0, 0, 0)),
            whole((2, COLS, COLS)),
        ],
        out_specs=block,
        out_shape=jax.ShapeDtypeStruct((MEMBERS, ROWS, COLS), F32),
        input_output_aliases={0: 0},
        compiler_params=PARAMS,
        cost_estimate=cost(10**9, 6 * 2**20),
        name="backward_edge",
    )(grad, top, bottom, edges, across)


def place_body(owner_ref, count_ref, value_ref, weight_ref, entry_ref, out_ref, used_ref):
    out_ref[...] = jnp.zeros_like(out_ref)

    def clear(i, carry):
        used_ref[i] = 0
        return carry

    lax.fori_loop(0, 128, clear, 0, unroll=8)
    lane = lax.broadcasted_iota(jnp.int32, (1, 256), 1)

    def put(b, carry):
        owner = owner_ref[b]
        slot = used_ref[owner]
        used_ref[owner] = slot + 1
        row = pl.ds(b, 1)
        weight = jnp.where(lane < count_ref[b], weight_ref[0, row, :], 0.0)
        out_ref[owner, pl.ds(slot, 1), :] = weight
        out_ref[owner, pl.ds(2 + slot, 1), :] = weight * value_ref[0, row, :]
        out_ref[owner, pl.ds(4 + slot, 1), :] = entry_ref[0, row, :].astype(F32)
        return carry

    lax.fori_loop(0, 112, put, 0, unroll=4)


def place(owner, count, value, weight, entry):
    smem = pl.BlockSpec(memory_space=pltpu.SMEM)
    vmem = pl.BlockSpec(memory_space=pltpu.VMEM)
    return pl.pallas_call(
        place_body,
        in_specs=[smem, smem, vmem, vmem, vmem],
        out_specs=vmem,
        out_shape=jax.ShapeDtypeStruct((128, 8, 256), F32),
        scratch_shapes=[pltpu.SMEM((128,), jnp.int32)],
        compiler_params=PARAMS,
        cost_estimate=cost(10**6, 2 * 2**20),
        name="place_blocks",
    )(owner, count, value, weight, entry)


SOURCES = 16


def tables_body(got_ref, w_ref, v_ref, acc):
    step = pl.program_id(0)

    @pl.when(step == 0)
    def _():
        acc[...] = jnp.zeros_like(acc)

    index = lax.broadcasted_iota(jnp.int32, (16, 512), 0).astype(F32).astype(BF16)
    one = jnp.ones((16, 512), BF16)
    zero = jnp.zeros((16, 512), BF16)

    def rows16(value):
        return jnp.broadcast_to(value, (16, 512)).astype(BF16)

    def source(s, carry):
        def line(at):
            return jnp.concatenate([got_ref[s, at : at + 1, :], got_ref[s, at + 1 : at + 2, :]], axis=1)

        weight, value, entry = line(0), line(2), line(4)
        half_row = jnp.floor(entry * (1.0 / 256.0))
        low = entry - 256.0 * half_row
        row = jnp.floor(half_row * 0.5)
        high = row + 16.0 * (half_row - 2.0 * row)
        low_at = rows16(low) - index
        high_at = rows16(high) - index
        left = []
        for quantity in (weight, value):
            first = quantity.astype(BF16).astype(F32)
            for term in (first, quantity - first):
                spread = rows16(term)
                for part in range(2):
                    left.append(jnp.where(high_at == 16.0 * part, spread, zero))
        right = [jnp.where(low_at == 16.0 * part, one, zero) for part in range(16)]
        acc[...] += lax.dot_general(
            jnp.concatenate(left, axis=0),
            jnp.concatenate(right, axis=0),
            (((1,), (1,)), ((), ())),
            preferred_element_type=F32,
        )
        return carry

    lax.fori_loop(0, SOURCES, source, 0)

    @pl.when(step == pl.num_programs(0) - 1)
    def _():
        for ref, base in ((w_ref, 0), (v_ref, 64)):
            total = acc[base : base + 32] + acc[base + 32 : base + 64]
            for field in range(2):
                at = 8 * field
                ref[field, :, 0:256] = total[at : at + 8]
                ref[field, :, 256:512] = total[16 + at : 24 + at]


def tables(got):
    piece = jax.ShapeDtypeStruct((2, SUB, COLS), F32)
    return pl.pallas_call(
        tables_body,
        grid=(128 // SOURCES,),
        in_specs=[pl.BlockSpec((SOURCES, 8, 256), lambda i: (i, 0, 0))],
        out_specs=[whole((2, SUB, COLS))] * 2,
        out_shape=[piece, piece],
        scratch_shapes=[pltpu.VMEM((128, 256), F32)],
        compiler_params=PARAMS,
        cost_estimate=cost(8 * 10**9, 2**20),
        name="weight_tables",
    )(got)


UP = [(0, 1), (1, 2), (2, 3)]
DOWN = [(1, 0), (2, 1), (3, 2)]
CORE = [(m, m ^ 1) for m in range(32)]


def along_z(step):
    return [(m, (m + 8 * step) % 32) for m in range(32)]


def along_x(step):
    return [(m, (m // 8) * 8 + ((m // 2) + step) % 4 * 2 + m % 2) for m in range(32)]


def exchange(bottom_rows, top_rows):
    return lax.ppermute(bottom_rows, "region", UP), lax.ppermute(top_rows, "region", DOWN)


def body(
    member_perts, alpha, background, obs_value, obs_weight, observed_subtile_entry, block_owner, block_count
):
    down = jnp.asarray(band(ROWS))
    across = jnp.asarray(band(COLS))
    vt, vb = [jnp.asarray(v) for v in edge_bands()]
    top, bottom = exchange(alpha[:, ROWS - EDGE :], alpha[:, :EDGE])
    send = place(block_owner[0, :, 0], block_count[0], obs_value, obs_weight, observed_subtile_entry)
    got = lax.all_to_all(send, ("region", "member"), split_axis=0, concat_axis=0, tiled=True)
    term = forward(alpha, member_perts, down, across)
    mine, other = forward_edge(term, top, bottom, member_perts, vt, vb, across)
    theirs = lax.ppermute(other, "member", CORE)
    keep, *sends = stage_z(mine, theirs)
    recv = [lax.ppermute(v, "member", along_z(s + 1)) for s, v in enumerate(sends)]
    keep, *sends = stage_x(keep, recv)
    recv = [lax.ppermute(v, "member", along_x(s + 1)) for s, v in enumerate(sends)]
    w_table, v_table = tables(got)
    adjoint = adjoint_of(background, keep, recv, w_table, v_table)
    recv = [lax.ppermute(adjoint, "member", along_x(s)) for s in (1, 2, 3)]
    line = gather_x(adjoint, recv)
    mine = [line] + [lax.ppermute(line, "member", along_z(s)) for s in (1, 2, 3)]
    other = [lax.ppermute(v, "member", CORE) for v in mine]
    adj, top_rows, bottom_rows = product_edge(mine, other, member_perts)
    top, bottom = exchange(bottom_rows, top_rows)
    grad = backward(alpha, member_perts, adj.reshape(2, ROWS, COLS), down, across)
    return backward_edge(grad, top, bottom, jnp.stack([vt, vb]), across)


def solution(mesh):
    placed = (
        P("member", None, "region", None),
        P("member", "region", None),
        P(None, ("region", "member"), None),
        P(("region", "member"), None, None),
        P(("region", "member"), None, None),
        P(("region", "member"), None, None),
        P(("region", "member"), None, None),
        P(("region", "member"), None),
    )
    return jax.shard_map(
        body, mesh=mesh, in_specs=placed, out_specs=P("member", "region", None), check_vma=False
    )
```

```python
import math

import jax
import jax.numpy as jnp
import ml_dtypes
import numpy as np
from jax import lax
from jax.experimental import pallas as pl
from jax.experimental.pallas import tpu as pltpu
from jax.sharding import PartitionSpec as P

HALF = 31
LENGTH_SCALE = 16.0
MEMBERS = 8
ROWS = 256
COLS = 512
EDGE = 32
SUB = 8
ENS_SCALE = 1.0 / math.sqrt(255.0)
F32 = jnp.float32
BF16 = jnp.bfloat16
PARAMS = pltpu.CompilerParams(vmem_limit_bytes=28 * 1024 * 1024)
STREAM = pltpu.CompilerParams(vmem_limit_bytes=58 * 1024 * 1024)
FORWARD = pltpu.CompilerParams(vmem_limit_bytes=52 * 1024 * 1024)
BACKWARD = pltpu.CompilerParams(vmem_limit_bytes=51 * 1024 * 1024)


def taps(offset):
    whole = np.arange(-HALF, HALF + 1).astype(np.float64)
    raw = np.exp(-whole * whole / (2.0 * LENGTH_SCALE**2))
    kernel = np.exp(-(offset.astype(np.float64) ** 2) / (2.0 * LENGTH_SCALE**2))
    return np.where(np.abs(offset) <= HALF, kernel / np.sqrt(np.sum(raw * raw)), 0.0)


def split_const(matrix):
    high = matrix.astype(ml_dtypes.bfloat16)
    low = (matrix - high.astype(np.float64)).astype(ml_dtypes.bfloat16)
    return high, low


def stack_terms(high, low, axis):
    return np.concatenate([high, high, low], axis=axis)


def band(size):
    index = np.arange(size)
    return taps(index[None, :] - index[:, None])


def constants():
    index = np.arange(EDGE)
    eye = np.eye(MEMBERS)
    top = np.kron(eye, taps(index[None, :] - EDGE - index[:, None]))
    bottom = np.kron(eye, taps(index[None, :] + EDGE - index[:, None]))
    downs = [stack_terms(*split_const(v), 1) for v in (band(ROWS), top, bottom)]
    wide = band(COLS)
    blocks = [wide[128 * i : 128 * i + 384, 256 * i : 256 * i + 256] for i in range(2)]
    across = np.stack([stack_terms(*split_const(v), 0) for v in blocks])
    return jnp.asarray(downs[0]), jnp.asarray(np.stack(downs[1:])), jnp.asarray(across)


def split(value):
    high = value.astype(BF16)
    return high, (value - high.astype(F32)).astype(BF16)


def mm(a, b):
    return jnp.dot(a, b, preferred_element_type=F32)


def terms(value, axis):
    high, low = split(value)
    return jnp.concatenate([high, low, high], axis=axis)


def down_rows(values, downs):
    return jnp.concatenate([mm(down, terms(value, 0)) for value, down in zip(values, downs)], axis=0)


def across_columns(rows, across_ref):
    high, low = split(rows)
    parts = []
    for block in range(2):
        k = slice(128 * block, 128 * block + 384)
        parts.append(mm(jnp.concatenate([high[:, k], low[:, k], high[:, k]], axis=1), across_ref[block]))
    return jnp.concatenate(parts, axis=1)


def conv(values, downs, across_ref):
    return across_columns(down_rows(values, downs), across_ref)


def whole(shape):
    return pl.BlockSpec(shape, lambda *_: (0,) * len(shape))


def cost(flops, nbytes):
    return pl.CostEstimate(flops=flops, bytes_accessed=nbytes, transcendentals=0)


VMEM = pl.BlockSpec(memory_space=pltpu.VMEM)
SMEM = pl.BlockSpec(memory_space=pltpu.SMEM)
HBM = pl.BlockSpec(memory_space=pltpu.HBM)
EDGES = (MEMBERS, EDGE, COLS)
PERTS_EDGES = (MEMBERS, 2, EDGE, COLS)
PIECES = (16, 2, SUB, COLS)


def out(shape, dtype=F32):
    return jax.ShapeDtypeStruct(shape, dtype)


def place_body(
    owner_hbm, count_hbm, value_hbm, weight_hbm, entry_hbm, alpha_hbm, perts_hbm,
    send_ref, first_ref, last_ref, perts_first_ref, perts_last_ref, owner_ref, count_ref, value_ref, weight_ref, entry_ref, used_ref, sems,
):
    pairs = [
        (owner_hbm, owner_ref), (count_hbm, count_ref),
        (value_hbm, value_ref), (weight_hbm, weight_ref), (entry_hbm, entry_ref),
        (alpha_hbm.at[:, :EDGE, :], first_ref), (alpha_hbm.at[:, ROWS - EDGE :, :], last_ref),
        (perts_hbm.at[:, :, :EDGE, :], perts_first_ref), (perts_hbm.at[:, :, ROWS - EDGE :, :], perts_last_ref),
    ]
    copies = [pltpu.make_async_copy(src, dst, sems.at[i]) for i, (src, dst) in enumerate(pairs)]
    for copy in copies:
        copy.start()
    send_ref[...] = jnp.zeros_like(send_ref)

    def clear(i, carry):
        used_ref[i] = 0
        return carry

    lax.fori_loop(0, 128, clear, 0, unroll=8)
    lane = lax.broadcasted_iota(jnp.int32, (1, 256), 1)
    for copy in copies[:5]:
        copy.wait()

    def put(b, carry):
        owner = owner_ref[b]
        slot = used_ref[owner]
        used_ref[owner] = slot + 1
        row = pl.ds(b, 1)
        weight = jnp.where(lane < count_ref[b], weight_ref[0, row, :], 0.0)
        put_at = pl.ds(slot, 1)
        send_ref[owner, put_at, 0:256] = weight
        send_ref[owner, put_at, 256:512] = weight * value_ref[0, row, :]
        send_ref[owner, put_at, 512:768] = entry_ref[0, row, :].astype(F32)
        return carry

    lax.fori_loop(0, 112, put, 0, unroll=4)
    for copy in copies[5:]:
        copy.wait()


def place(owner, count, value, weight, entry, alpha, perts):
    return pl.pallas_call(
        place_body,
        in_specs=[HBM] * 7,
        out_specs=[VMEM] * 5,
        out_shape=[
            out((128, 2, 768)), out(EDGES), out(EDGES), out(PERTS_EDGES, BF16), out(PERTS_EDGES, BF16),
        ],
        scratch_shapes=[
            pltpu.SMEM(owner.shape, jnp.int32), pltpu.SMEM(count.shape, jnp.int32),
            pltpu.VMEM(value.shape, F32), pltpu.VMEM(value.shape, F32), pltpu.VMEM(value.shape, jnp.int32),
            pltpu.SMEM((128,), jnp.int32), pltpu.SemaphoreType.DMA((9,)),
        ],
        compiler_params=STREAM,
        cost_estimate=cost(10**9, 0),
        name="place",
    )(owner, count, value, weight, entry, alpha, perts)


GROUP = 4
FIELD = (2, 16, 2, SUB, COLS)


def member_copies(source, target, sems):
    return [pltpu.make_async_copy(source.at[k], target.at[k], sems.at[k]) for k in range(MEMBERS)]


def forward_body(
    alpha_hbm, perts_hbm, down_hbm, across_hbm, term_ref,
    alpha_ref, perts_ref, down_ref, across_ref, alpha_sems, perts_sems, const_sems,
):
    alpha_copies = member_copies(alpha_hbm, alpha_ref, alpha_sems)
    perts_copies = member_copies(perts_hbm, perts_ref, perts_sems)
    down_copy = pltpu.make_async_copy(down_hbm, down_ref, const_sems.at[0])
    across_copy = pltpu.make_async_copy(across_hbm, across_ref, const_sems.at[1])
    down_copy.start()
    for base in range(0, MEMBERS, GROUP):
        for k in range(base, base + GROUP):
            alpha_copies[k].start()
        if base == 0:
            across_copy.start()
        for k in range(base, base + GROUP):
            perts_copies[k].start()
    down_copy.wait()
    rows = None
    for base in range(0, MEMBERS + GROUP, GROUP):
        before = rows
        if base < MEMBERS:
            members = range(base, base + GROUP)
            for k in members:
                alpha_copies[k].wait()
        if base == GROUP:
            across_copy.wait()
        if base > 0:
            for k in range(base - GROUP, base):
                perts_copies[k].wait()
        if base < MEMBERS:
            rows = down_rows([alpha_ref[k] for k in members], [down_ref[...]] * GROUP)
        if base > 0:
            spread = across_columns(before, across_ref)
            for field in range(2):
                total = perts_ref[base - GROUP, field].astype(F32) * spread[:ROWS]
                for m in range(1, GROUP):
                    part = spread[ROWS * m : ROWS * (m + 1)]
                    total += perts_ref[base - GROUP + m, field].astype(F32) * part
                total = total.reshape(FIELD[1:])
                if base == GROUP:
                    term_ref[field] = total
                else:
                    term_ref[field] += total


def forward(alpha, perts, down, across):
    return pl.pallas_call(
        forward_body,
        in_specs=[HBM] * 4,
        out_specs=VMEM,
        out_shape=out(FIELD),
        scratch_shapes=[
            pltpu.VMEM(alpha.shape, F32), pltpu.VMEM(perts.shape, BF16),
            pltpu.VMEM(down.shape, BF16), pltpu.VMEM(across.shape, BF16),
            pltpu.SemaphoreType.DMA((MEMBERS,)), pltpu.SemaphoreType.DMA((MEMBERS,)),
            pltpu.SemaphoreType.DMA((2,)),
        ],
        compiler_params=FORWARD,
        cost_estimate=cost(10**6, 0),
        name="forward",
    )(alpha, perts, down, across)


def forward_edge_body(
    term_ref, top_ref, bottom_ref, perts_first_ref, perts_last_ref, down_ref, across_ref, mine_ref, other_ref
):
    core = lax.rem(lax.axis_index("member"), 2)
    for field in range(2):
        mine_ref[:, field] = term_ref[field, :, core]
        other_ref[:, field] = term_ref[field, :, 1 - core]
    halo = [ref[...].reshape(MEMBERS * EDGE, COLS) for ref in (top_ref, bottom_ref)]
    spread = conv(halo, [down_ref[0], down_ref[1]], across_ref).reshape((2,) + EDGES)
    for side, p_ref in enumerate((perts_first_ref, perts_last_ref)):
        at = slice(14 * side, 14 * side + 2)
        for field in range(2):
            total = jnp.sum(p_ref[:, field].astype(F32) * spread[side], axis=0).reshape(2, 2, SUB, COLS)
            even = core == 0
            mine_ref[at, field] += jnp.where(even, total[:, 0], total[:, 1])
            other_ref[at, field] += jnp.where(even, total[:, 1], total[:, 0])


def forward_edge(term, top, bottom, perts_first, perts_last, down, across):
    return pl.pallas_call(
        forward_edge_body,
        in_specs=[VMEM] * 7,
        out_specs=[VMEM] * 2,
        out_shape=[out(PIECES), out(PIECES)],
        compiler_params=PARAMS,
        cost_estimate=cost(10**9, 6 * 2**20),
        name="forward_edge",
    )(term, top, bottom, perts_first, perts_last, down, across)


def adjoint_body(back_ref, got_ref, w_ref, v_ref, out_ref):
    state = back_ref[...] + ENS_SCALE * jnp.sum(got_ref[...], axis=0)
    out_ref[...] = jnp.broadcast_to((state * w_ref[...] - v_ref[...])[None], PIECES)


def adjoint_of(back, got, w, v):
    return pl.pallas_call(
        adjoint_body, in_specs=[VMEM] * 4, out_specs=VMEM, out_shape=out(PIECES), compiler_params=PARAMS,
        cost_estimate=cost(10**5, 2**20), name="adjoint",
    )(back, got, w, v)


def perts_edges_body(first_in_ref, last_in_ref, anchor_ref, first_ref, last_ref):
    first_ref[...] = first_in_ref[...].astype(F32)
    last_ref[...] = last_in_ref[...].astype(F32)


def perts_edges(first, last, anchor):
    return pl.pallas_call(
        perts_edges_body, in_specs=[VMEM, VMEM, HBM], out_specs=[VMEM] * 2,
        out_shape=[out(PERTS_EDGES), out(PERTS_EDGES)],
        compiler_params=PARAMS, cost_estimate=cost(10**10, 0), name="perts_edges",
    )(first, last, anchor)


def assemble_body(mine_ref, other_ref, adj_ref, first_ref, last_ref):
    core = lax.rem(lax.axis_index("member"), 2)
    for field in range(2):
        adj_ref[field, :, core] = mine_ref[:, field]
        adj_ref[field, :, 1 - core] = other_ref[:, field]
    for field in range(2):
        first_ref[field] = adj_ref[field, :2]
        last_ref[field] = adj_ref[field, 14:]


def assemble(mine, other):
    edge = out((2, 2, 2, SUB, COLS))
    return pl.pallas_call(
        assemble_body, in_specs=[VMEM] * 2, out_specs=[VMEM] * 3,
        out_shape=[out((2, 16, 2, SUB, COLS)), edge, edge], compiler_params=PARAMS,
        cost_estimate=cost(10**5, 2 * 2**20), name="assemble",
    )(mine, other)


def backward_body(
    alpha_hbm, perts_hbm, adj_ref, down_hbm, across_hbm, grad_hbm, edge_ref,
    scr, alpha_ref, perts_ref, down_ref, across_ref, alpha_sems, perts_sems, grad_sems, const_sems,
):
    alpha_copies = member_copies(alpha_hbm, alpha_ref, alpha_sems)
    perts_copies = member_copies(perts_hbm, perts_ref, perts_sems)
    copies = member_copies(scr, grad_hbm, grad_sems)
    down_copy = pltpu.make_async_copy(down_hbm, down_ref, const_sems.at[0])
    across_copy = pltpu.make_async_copy(across_hbm, across_ref, const_sems.at[1])
    down_copy.start()
    for base in range(0, MEMBERS, GROUP):
        for k in range(base, base + GROUP):
            perts_copies[k].start()
        if base == 0:
            across_copy.start()
        for k in range(base, base + GROUP):
            alpha_copies[k].start()
    down_copy.wait()
    rows = None
    for base in range(0, MEMBERS + GROUP, GROUP):
        before = rows
        if base < MEMBERS:
            for k in range(base, base + GROUP):
                perts_copies[k].wait()
        if base == GROUP:
            across_copy.wait()
        if base > 0:
            for k in range(base - GROUP, base):
                alpha_copies[k].wait()
        if base < MEMBERS:
            products = []
            for k in range(base, base + GROUP):
                product = perts_ref[k, 0].astype(F32) * adj_ref[0]
                products.append(product + perts_ref[k, 1].astype(F32) * adj_ref[1])
            rows = down_rows(products, [down_ref[...]] * GROUP)
        if base > 0:
            spread = across_columns(before, across_ref)
            for m in range(GROUP):
                k = base - GROUP + m
                scr[k] = alpha_ref[k] + ENS_SCALE * spread[ROWS * m : ROWS * (m + 1)]
                edge_ref[0, k] = scr[k, :EDGE]
                edge_ref[1, k] = scr[k, ROWS - EDGE :]
            for k in range(base - GROUP, base):
                copies[k].start()
    for copy in copies:
        copy.wait()


def backward(alpha, perts, adj, down, across):
    return pl.pallas_call(
        backward_body,
        in_specs=[HBM, HBM, VMEM, HBM, HBM],
        out_specs=[HBM, VMEM],
        out_shape=[out(alpha.shape), out((2,) + EDGES)],
        scratch_shapes=[
            pltpu.VMEM(alpha.shape, F32), pltpu.VMEM(alpha.shape, F32), pltpu.VMEM(perts.shape, BF16),
            pltpu.VMEM(down.shape, BF16), pltpu.VMEM(across.shape, BF16),
            pltpu.SemaphoreType.DMA((MEMBERS,)), pltpu.SemaphoreType.DMA((MEMBERS,)),
            pltpu.SemaphoreType.DMA((MEMBERS,)), pltpu.SemaphoreType.DMA((2,)),
        ],
        compiler_params=BACKWARD,
        cost_estimate=cost(10**6, 0),
        name="backward_own",
    )(alpha, perts, adj, down, across)


def backward_edge_body(
    grad_hbm, edge_ref, pt_ref, pb_ref, at_ref, ab_ref, down_ref, across_ref, out_hbm, scr, sems
):
    products = []
    for p_ref, a_ref in ((pt_ref, at_ref), (pb_ref, ab_ref)):
        first, second = [a_ref[field].reshape(1, EDGE, COLS) for field in range(2)]
        products.append((p_ref[:, 0] * first + p_ref[:, 1] * second).reshape(MEMBERS * EDGE, COLS))
    spread = conv(products, [down_ref[0], down_ref[1]], across_ref).reshape((2,) + EDGES)
    copies = []
    for side in range(2):
        scr[side] = edge_ref[side] + ENS_SCALE * spread[side]
        at = (ROWS - EDGE) * side
        copies.append(pltpu.make_async_copy(scr.at[side], out_hbm.at[:, at : at + EDGE, :], sems.at[side]))
        copies[side].start()
    for copy in copies:
        copy.wait()


def backward_edge(grad, edge, pt, pb, at, ab, down, across):
    return pl.pallas_call(
        backward_edge_body,
        in_specs=[HBM] + [VMEM] * 7,
        out_specs=HBM,
        out_shape=out(grad.shape),
        input_output_aliases={0: 0},
        scratch_shapes=[pltpu.VMEM((2,) + EDGES, F32), pltpu.SemaphoreType.DMA((2,))],
        compiler_params=PARAMS,
        cost_estimate=cost(10**9, 6 * 2**20),
        name="backward_edge",
    )(grad, edge, pt, pb, at, ab, down, across)


SOURCES = 16
HIGH = 64
LOW = 128


def tables_body(got_ref, w_ref, v_ref, acc):
    step = pl.program_id(0)

    @pl.when(step == 0)
    def _():
        acc[...] = jnp.zeros_like(acc)

    index = lax.broadcasted_iota(jnp.int32, (16, 512), 0).astype(F32).astype(BF16)
    one = jnp.ones((16, 512), BF16)
    zero = jnp.zeros((16, 512), BF16)

    def rows16(value):
        return jnp.broadcast_to(value, (16, 512)).astype(BF16)

    def source(s, carry):
        def line(at):
            return jnp.concatenate([got_ref[s, 0:1, at : at + 256], got_ref[s, 1:2, at : at + 256]], axis=1)

        weight, value, entry = line(0), line(256), line(512)
        chunk = jnp.floor(entry * (1.0 / LOW))
        row = jnp.floor(chunk * 0.25)
        low_at = rows16(entry - LOW * chunk) - index
        high_at = rows16(row + 16.0 * (chunk - 4.0 * row)) - index
        hits = [high_at == 16.0 * part for part in range(HIGH // 16)]
        left = []
        for quantity in (weight, value):
            first = quantity.astype(BF16).astype(F32)
            for term in (first, quantity - first):
                spread = rows16(term)
                left += [jnp.where(hit, spread, zero) for hit in hits]
        right = [jnp.where(low_at == 16.0 * part, one, zero) for part in range(LOW // 16)]
        acc[...] += lax.dot_general(
            jnp.concatenate(left, axis=0),
            jnp.concatenate(right, axis=0),
            (((1,), (1,)), ((), ())),
            preferred_element_type=F32,
        )
        return carry

    lax.fori_loop(0, SOURCES, source, 0, unroll=8)

    @pl.when(step == pl.num_programs(0) - 1)
    def _():
        for ref, base in ((w_ref, 0), (v_ref, 2 * HIGH)):
            total = acc[base : base + HIGH] + acc[base + HIGH : base + 2 * HIGH]
            for field in range(2):
                for chunk in range(4):
                    at = 16 * chunk + 8 * field
                    ref[field, :, LOW * chunk : LOW * (chunk + 1)] = total[at : at + 8]


def tables(got):
    piece = jax.ShapeDtypeStruct((2, SUB, COLS), F32)
    return pl.pallas_call(
        tables_body,
        grid=(128 // SOURCES,),
        in_specs=[pl.BlockSpec((SOURCES, 2, 768), lambda i: (i, 0, 0))],
        out_specs=[whole((2, SUB, COLS))] * 2,
        out_shape=[piece, piece],
        scratch_shapes=[pltpu.VMEM((4 * HIGH, LOW), F32)],
        compiler_params=PARAMS,
        cost_estimate=cost(12 * 10**9, 2**20),
        name="weight_tables",
    )(got)


UP = [(0, 1), (1, 2), (2, 3)]
DOWN = [(1, 0), (2, 1), (3, 2)]
CORE = [(m, m ^ 1) for m in range(32)]
SAME_CORE = [[2 * q + core for q in range(16)] for core in range(2)]


def exchange(last, first):
    return lax.ppermute(last, "region", UP), lax.ppermute(first, "region", DOWN)


def among_sixteen(pieces):
    return lax.all_to_all(
        pieces, "member", split_axis=0, concat_axis=0, axis_index_groups=SAME_CORE, tiled=True
    )


def body(
    member_perts, alpha, background, obs_value, obs_weight, observed_subtile_entry, block_owner, block_count
):
    down, edge_downs, across = constants()
    send, first, last, perts_first, perts_last = place(
        block_owner[0, :, 0], block_count[0], obs_value, obs_weight, observed_subtile_entry, alpha, member_perts
    )
    top, bottom = exchange(last, first)
    term = forward(alpha, member_perts, down, across)
    got = lax.all_to_all(send, ("region", "member"), split_axis=0, concat_axis=0, tiled=True)
    mine, other = forward_edge(term, top, bottom, perts_first, perts_last, edge_downs, across)
    pieces = among_sixteen(mine + lax.ppermute(other, "member", CORE))
    w_table, v_table = tables(got)
    adjoint = adjoint_of(background, pieces, w_table, v_table)
    mine = among_sixteen(adjoint)
    first, last = perts_edges(perts_first, perts_last, adjoint)
    perts_top, perts_bottom = exchange(last, first)
    adj, first, last = assemble(mine, lax.ppermute(mine, "member", CORE))
    adj_top, adj_bottom = exchange(last, first)
    grad, edge = backward(alpha, member_perts, adj.reshape(2, ROWS, COLS), down, across)
    return backward_edge(grad, edge, perts_top, perts_bottom, adj_top, adj_bottom, edge_downs, across)


def solution(mesh):
    placed = (
        P("member", None, "region", None),
        P("member", "region", None),
        P(None, ("region", "member"), None),
        P(("region", "member"), None, None),
        P(("region", "member"), None, None),
        P(("region", "member"), None, None),
        P(("region", "member"), None, None),
        P(("region", "member"), None),
    )
    return jax.shard_map(
        body, mesh=mesh, in_specs=placed, out_specs=P("member", "region", None), check_vma=False
    )
```

```python
import math

import jax
import jax.numpy as jnp
import ml_dtypes
import numpy as np
from jax import lax
from jax.experimental import pallas as pl
from jax.experimental.pallas import tpu as pltpu
from jax.sharding import PartitionSpec as P

HALF = 31
LENGTH_SCALE = 16.0
MEMBERS = 8
ROWS = 256
COLS = 512
EDGE = 32
SUB = 8
ENS_SCALE = 1.0 / math.sqrt(255.0)
F32 = jnp.float32
BF16 = jnp.bfloat16
PARAMS = pltpu.CompilerParams(vmem_limit_bytes=28 * 1024 * 1024)
STREAM = pltpu.CompilerParams(vmem_limit_bytes=58 * 1024 * 1024)
FORWARD = pltpu.CompilerParams(vmem_limit_bytes=52 * 1024 * 1024)
BACKWARD = pltpu.CompilerParams(vmem_limit_bytes=51 * 1024 * 1024)


def taps(offset):
    whole = np.arange(-HALF, HALF + 1).astype(np.float64)
    raw = np.exp(-whole * whole / (2.0 * LENGTH_SCALE**2))
    kernel = np.exp(-(offset.astype(np.float64) ** 2) / (2.0 * LENGTH_SCALE**2))
    return np.where(np.abs(offset) <= HALF, kernel / np.sqrt(np.sum(raw * raw)), 0.0)


def split_const(matrix):
    high = matrix.astype(ml_dtypes.bfloat16)
    low = (matrix - high.astype(np.float64)).astype(ml_dtypes.bfloat16)
    return high, low


def stack_terms(high, low, axis):
    return np.concatenate([high, high, low], axis=axis)


def band(size):
    index = np.arange(size)
    return taps(index[None, :] - index[:, None])


def constants():
    index = np.arange(EDGE)
    eye = np.eye(MEMBERS)
    top = np.kron(eye, taps(index[None, :] - EDGE - index[:, None]))
    bottom = np.kron(eye, taps(index[None, :] + EDGE - index[:, None]))
    downs = [stack_terms(*split_const(v), 1) for v in (band(ROWS), top, bottom)]
    wide = band(COLS)
    blocks = [wide[128 * i : 128 * i + 384, 256 * i : 256 * i + 256] for i in range(2)]
    across = np.stack([stack_terms(*split_const(v), 0) for v in blocks])
    return jnp.asarray(downs[0]), jnp.asarray(np.stack(downs[1:])), jnp.asarray(across)


def split(value):
    high = value.astype(BF16)
    return high, (value - high.astype(F32)).astype(BF16)


def mm(a, b):
    return jnp.dot(a, b, preferred_element_type=F32)


def terms(value, axis):
    high, low = split(value)
    return jnp.concatenate([high, low, high], axis=axis)


def down_rows(values, downs):
    return jnp.concatenate([mm(down, terms(value, 0)) for value, down in zip(values, downs)], axis=0)


def across_columns(rows, across_ref):
    high, low = split(rows)
    parts = []
    for block in range(2):
        k = slice(128 * block, 128 * block + 384)
        parts.append(mm(jnp.concatenate([high[:, k], low[:, k], high[:, k]], axis=1), across_ref[block]))
    return jnp.concatenate(parts, axis=1)


def conv(values, downs, across_ref):
    return across_columns(down_rows(values, downs), across_ref)


def whole(shape):
    return pl.BlockSpec(shape, lambda *_: (0,) * len(shape))


def cost(flops, nbytes):
    return pl.CostEstimate(flops=flops, bytes_accessed=nbytes, transcendentals=0)


VMEM = pl.BlockSpec(memory_space=pltpu.VMEM)
SMEM = pl.BlockSpec(memory_space=pltpu.SMEM)
HBM = pl.BlockSpec(memory_space=pltpu.HBM)
EDGES = (MEMBERS, EDGE, COLS)
PERTS_EDGES = (MEMBERS, 2, EDGE, COLS)
PIECES = (16, 2, SUB, COLS)


def out(shape, dtype=F32):
    return jax.ShapeDtypeStruct(shape, dtype)


def place_body(
    owner_hbm, count_hbm, value_hbm, weight_hbm, entry_hbm, alpha_hbm, perts_hbm,
    send_ref, first_ref, last_ref, perts_first_ref, perts_last_ref, owner_ref, count_ref, value_ref, weight_ref, entry_ref, used_ref, sems,
):
    pairs = [
        (owner_hbm, owner_ref), (count_hbm, count_ref),
        (value_hbm, value_ref), (weight_hbm, weight_ref), (entry_hbm, entry_ref),
        (alpha_hbm.at[:, :EDGE, :], first_ref), (alpha_hbm.at[:, ROWS - EDGE :, :], last_ref),
        (perts_hbm.at[:, :, :EDGE, :], perts_first_ref), (perts_hbm.at[:, :, ROWS - EDGE :, :], perts_last_ref),
    ]
    copies = [pltpu.make_async_copy(src, dst, sems.at[i]) for i, (src, dst) in enumerate(pairs)]
    for copy in copies:
        copy.start()
    send_ref[...] = jnp.zeros_like(send_ref)

    def clear(i, carry):
        used_ref[i] = 0
        return carry

    lax.fori_loop(0, 128, clear, 0, unroll=8)
    lane = lax.broadcasted_iota(jnp.int32, (1, 256), 1)
    for copy in copies[:5]:
        copy.wait()

    def put(b, carry):
        owner = owner_ref[b]
        slot = used_ref[owner]
        used_ref[owner] = slot + 1
        row = pl.ds(b, 1)
        weight = jnp.where(lane < count_ref[b], weight_ref[0, row, :], 0.0)
        put_at = pl.ds(slot, 1)
        send_ref[owner, put_at, 0:256] = weight
        send_ref[owner, put_at, 256:512] = weight * value_ref[0, row, :]
        send_ref[owner, put_at, 512:768] = entry_ref[0, row, :].astype(F32)
        return carry

    lax.fori_loop(0, 112, put, 0, unroll=4)
    for copy in copies[5:]:
        copy.wait()


def place(owner, count, value, weight, entry, alpha, perts):
    return pl.pallas_call(
        place_body,
        in_specs=[HBM] * 7,
        out_specs=[VMEM] * 5,
        out_shape=[
            out((128, 2, 768)), out(EDGES), out(EDGES), out(PERTS_EDGES, BF16), out(PERTS_EDGES, BF16),
        ],
        scratch_shapes=[
            pltpu.SMEM(owner.shape, jnp.int32), pltpu.SMEM(count.shape, jnp.int32),
            pltpu.VMEM(value.shape, F32), pltpu.VMEM(value.shape, F32), pltpu.VMEM(value.shape, jnp.int32),
            pltpu.SMEM((128,), jnp.int32), pltpu.SemaphoreType.DMA((9,)),
        ],
        compiler_params=STREAM,
        cost_estimate=cost(10**9, 0),
        name="place",
    )(owner, count, value, weight, entry, alpha, perts)


GROUP = 4
FIELD = (2, 16, 2, SUB, COLS)


def member_copies(source, target, sems):
    return [pltpu.make_async_copy(source.at[k], target.at[k], sems.at[k]) for k in range(MEMBERS)]


def forward_body(
    alpha_hbm, perts_hbm, down_hbm, across_hbm, term_ref,
    alpha_ref, perts_ref, down_ref, across_ref, alpha_sems, perts_sems, const_sems,
):
    alpha_copies = member_copies(alpha_hbm, alpha_ref, alpha_sems)
    perts_copies = member_copies(perts_hbm, perts_ref, perts_sems)
    down_copy = pltpu.make_async_copy(down_hbm, down_ref, const_sems.at[0])
    across_copy = pltpu.make_async_copy(across_hbm, across_ref, const_sems.at[1])
    down_copy.start()
    for base in range(0, MEMBERS, GROUP):
        for k in range(base, base + GROUP):
            alpha_copies[k].start()
        if base == 0:
            across_copy.start()
        for k in range(base, base + GROUP):
            perts_copies[k].start()
    down_copy.wait()
    rows = None
    for base in range(0, MEMBERS + GROUP, GROUP):
        before = rows
        if base < MEMBERS:
            members = range(base, base + GROUP)
            for k in members:
                alpha_copies[k].wait()
        if base == GROUP:
            across_copy.wait()
        if base > 0:
            for k in range(base - GROUP, base):
                perts_copies[k].wait()
        if base < MEMBERS:
            rows = down_rows([alpha_ref[k] for k in members], [down_ref[...]] * GROUP)
        if base > 0:
            spread = across_columns(before, across_ref)
            for field in range(2):
                total = perts_ref[base - GROUP, field].astype(F32) * spread[:ROWS]
                for m in range(1, GROUP):
                    part = spread[ROWS * m : ROWS * (m + 1)]
                    total += perts_ref[base - GROUP + m, field].astype(F32) * part
                total = total.reshape(FIELD[1:])
                if base == GROUP:
                    term_ref[field] = total
                else:
                    term_ref[field] += total


def forward(alpha, perts, down, across):
    return pl.pallas_call(
        forward_body,
        in_specs=[HBM] * 4,
        out_specs=VMEM,
        out_shape=out(FIELD),
        scratch_shapes=[
            pltpu.VMEM(alpha.shape, F32), pltpu.VMEM(perts.shape, BF16),
            pltpu.VMEM(down.shape, BF16), pltpu.VMEM(across.shape, BF16),
            pltpu.SemaphoreType.DMA((MEMBERS,)), pltpu.SemaphoreType.DMA((MEMBERS,)),
            pltpu.SemaphoreType.DMA((2,)),
        ],
        compiler_params=FORWARD,
        cost_estimate=cost(10**6, 0),
        name="forward",
    )(alpha, perts, down, across)


def forward_edge_body(
    term_ref, top_ref, bottom_ref, perts_first_ref, perts_last_ref, down_ref, across_ref, mine_ref, other_ref
):
    core = lax.rem(lax.axis_index("member"), 2)
    for field in range(2):
        mine_ref[:, field] = term_ref[field, :, core]
        other_ref[:, field] = term_ref[field, :, 1 - core]
    halo = [ref[...].reshape(MEMBERS * EDGE, COLS) for ref in (top_ref, bottom_ref)]
    spread = conv(halo, [down_ref[0], down_ref[1]], across_ref).reshape((2,) + EDGES)
    for side, p_ref in enumerate((perts_first_ref, perts_last_ref)):
        at = slice(14 * side, 14 * side + 2)
        for field in range(2):
            total = jnp.sum(p_ref[:, field].astype(F32) * spread[side], axis=0).reshape(2, 2, SUB, COLS)
            even = core == 0
            mine_ref[at, field] += jnp.where(even, total[:, 0], total[:, 1])
            other_ref[at, field] += jnp.where(even, total[:, 1], total[:, 0])


def forward_edge(term, top, bottom, perts_first, perts_last, down, across):
    return pl.pallas_call(
        forward_edge_body,
        in_specs=[VMEM] * 7,
        out_specs=[VMEM] * 2,
        out_shape=[out(PIECES), out(PIECES)],
        compiler_params=PARAMS,
        cost_estimate=cost(10**9, 6 * 2**20),
        name="forward_edge",
    )(term, top, bottom, perts_first, perts_last, down, across)


def adjoint_body(back_ref, got_ref, w_ref, v_ref, out_ref):
    state = back_ref[...] + ENS_SCALE * jnp.sum(got_ref[...], axis=0)
    out_ref[...] = jnp.broadcast_to((state * w_ref[...] - v_ref[...])[None], PIECES)


def adjoint_of(back, got, w, v):
    return pl.pallas_call(
        adjoint_body, in_specs=[VMEM] * 4, out_specs=VMEM, out_shape=out(PIECES), compiler_params=PARAMS,
        cost_estimate=cost(10**5, 2**20), name="adjoint",
    )(back, got, w, v)


def assemble_body(mine_ref, other_ref, perts_first_ref, perts_last_ref, adj_ref, first_ref, last_ref):
    core = lax.rem(lax.axis_index("member"), 2)
    for field in range(2):
        adj_ref[field, :, core] = mine_ref[:, field]
        adj_ref[field, :, 1 - core] = other_ref[:, field]
    for at, p_ref, edge_ref in ((0, perts_first_ref, first_ref), (14, perts_last_ref, last_ref)):
        rows = [adj_ref[field, at : at + 2].reshape(EDGE, COLS) for field in range(2)]
        for m in range(MEMBERS):
            edge_ref[m] = p_ref[m, 0].astype(F32) * rows[0] + p_ref[m, 1].astype(F32) * rows[1]


def assemble(mine, other, perts_first, perts_last):
    return pl.pallas_call(
        assemble_body, in_specs=[VMEM] * 4, out_specs=[VMEM] * 3,
        out_shape=[out(FIELD), out(EDGES), out(EDGES)], compiler_params=PARAMS,
        cost_estimate=cost(10**5, 2 * 2**20), name="assemble",
    )(mine, other, perts_first, perts_last)


def backward_body(
    alpha_hbm, perts_hbm, adj_ref, down_hbm, across_hbm, grad_hbm, edge_ref,
    scr, alpha_ref, perts_ref, down_ref, across_ref, alpha_sems, perts_sems, grad_sems, const_sems,
):
    alpha_copies = member_copies(alpha_hbm, alpha_ref, alpha_sems)
    perts_copies = member_copies(perts_hbm, perts_ref, perts_sems)
    copies = member_copies(scr, grad_hbm, grad_sems)
    down_copy = pltpu.make_async_copy(down_hbm, down_ref, const_sems.at[0])
    across_copy = pltpu.make_async_copy(across_hbm, across_ref, const_sems.at[1])
    down_copy.start()
    for base in range(0, MEMBERS, GROUP):
        for k in range(base, base + GROUP):
            perts_copies[k].start()
        if base == 0:
            across_copy.start()
        for k in range(base, base + GROUP):
            alpha_copies[k].start()
    down_copy.wait()
    rows = None
    for base in range(0, MEMBERS + GROUP, GROUP):
        before = rows
        if base < MEMBERS:
            for k in range(base, base + GROUP):
                perts_copies[k].wait()
        if base == GROUP:
            across_copy.wait()
        if base > 0:
            for k in range(base - GROUP, base):
                alpha_copies[k].wait()
        if base < MEMBERS:
            products = []
            for k in range(base, base + GROUP):
                product = perts_ref[k, 0].astype(F32) * adj_ref[0]
                products.append(product + perts_ref[k, 1].astype(F32) * adj_ref[1])
            rows = down_rows(products, [down_ref[...]] * GROUP)
        if base > 0:
            spread = across_columns(before, across_ref)
            for m in range(GROUP):
                k = base - GROUP + m
                scr[k] = alpha_ref[k] + ENS_SCALE * spread[ROWS * m : ROWS * (m + 1)]
                edge_ref[0, k] = scr[k, :EDGE]
                edge_ref[1, k] = scr[k, ROWS - EDGE :]
            for k in range(base - GROUP, base):
                copies[k].start()
    for copy in copies:
        copy.wait()


def backward(alpha, perts, adj, down, across):
    return pl.pallas_call(
        backward_body,
        in_specs=[HBM, HBM, VMEM, HBM, HBM],
        out_specs=[HBM, VMEM],
        out_shape=[out(alpha.shape), out((2,) + EDGES)],
        scratch_shapes=[
            pltpu.VMEM(alpha.shape, F32), pltpu.VMEM(alpha.shape, F32), pltpu.VMEM(perts.shape, BF16),
            pltpu.VMEM(down.shape, BF16), pltpu.VMEM(across.shape, BF16),
            pltpu.SemaphoreType.DMA((MEMBERS,)), pltpu.SemaphoreType.DMA((MEMBERS,)),
            pltpu.SemaphoreType.DMA((MEMBERS,)), pltpu.SemaphoreType.DMA((2,)),
        ],
        compiler_params=BACKWARD,
        cost_estimate=cost(10**6, 0),
        name="backward_own",
    )(alpha, perts, adj, down, across)


def backward_edge_body(grad_hbm, edge_ref, top_ref, bottom_ref, down_ref, across_ref, out_hbm, scr, sems):
    halo = [ref[...].reshape(MEMBERS * EDGE, COLS) for ref in (top_ref, bottom_ref)]
    spread = conv(halo, [down_ref[0], down_ref[1]], across_ref).reshape((2,) + EDGES)
    copies = []
    for side in range(2):
        scr[side] = edge_ref[side] + ENS_SCALE * spread[side]
        at = (ROWS - EDGE) * side
        copies.append(pltpu.make_async_copy(scr.at[side], out_hbm.at[:, at : at + EDGE, :], sems.at[side]))
        copies[side].start()
    for copy in copies:
        copy.wait()


def backward_edge(grad, edge, top, bottom, down, across):
    return pl.pallas_call(
        backward_edge_body,
        in_specs=[HBM] + [VMEM] * 5,
        out_specs=HBM,
        out_shape=out(grad.shape),
        input_output_aliases={0: 0},
        scratch_shapes=[pltpu.VMEM((2,) + EDGES, F32), pltpu.SemaphoreType.DMA((2,))],
        compiler_params=PARAMS,
        cost_estimate=cost(10**9, 6 * 2**20),
        name="backward_edge",
    )(grad, edge, top, bottom, down, across)


SOURCES = 128
HIGH = 64
LOW = 128


def tables_body(got_ref, w_ref, v_ref, acc):
    acc[...] = jnp.zeros_like(acc)
    index = lax.broadcasted_iota(jnp.int32, (16, 512), 0).astype(F32).astype(BF16)
    one = jnp.ones((16, 512), BF16)
    zero = jnp.zeros((16, 512), BF16)

    def rows16(value):
        return jnp.broadcast_to(value, (16, 512)).astype(BF16)

    def source(s, carry):
        def line(at):
            return jnp.concatenate([got_ref[s, 0:1, at : at + 256], got_ref[s, 1:2, at : at + 256]], axis=1)

        weight, value, entry = line(0), line(256), line(512)
        chunk = jnp.floor(entry * (1.0 / LOW))
        row = jnp.floor(chunk * 0.25)
        low_at = rows16(entry - LOW * chunk) - index
        high_at = rows16(row + 16.0 * (chunk - 4.0 * row)) - index
        hits = [high_at == 16.0 * part for part in range(HIGH // 16)]
        left = []
        for quantity in (weight, value):
            first = quantity.astype(BF16).astype(F32)
            for term in (first, quantity - first):
                spread = rows16(term)
                left += [jnp.where(hit, spread, zero) for hit in hits]
        right = [jnp.where(low_at == 16.0 * part, one, zero) for part in range(LOW // 16)]
        acc[...] += lax.dot_general(
            jnp.concatenate(left, axis=0),
            jnp.concatenate(right, axis=0),
            (((1,), (1,)), ((), ())),
            preferred_element_type=F32,
        )
        return carry

    lax.fori_loop(0, SOURCES, source, 0, unroll=16)
    for ref, base in ((w_ref, 0), (v_ref, 2 * HIGH)):
        total = acc[base : base + HIGH] + acc[base + HIGH : base + 2 * HIGH]
        for field in range(2):
            for chunk in range(4):
                at = 16 * chunk + 8 * field
                ref[field, :, LOW * chunk : LOW * (chunk + 1)] = total[at : at + 8]


def tables(got):
    piece = jax.ShapeDtypeStruct((2, SUB, COLS), F32)
    return pl.pallas_call(
        tables_body,
        in_specs=[VMEM],
        out_specs=[VMEM] * 2,
        out_shape=[piece, piece],
        scratch_shapes=[pltpu.VMEM((4 * HIGH, LOW), F32)],
        compiler_params=PARAMS,
        cost_estimate=cost(12 * 10**9, 2**20),
        name="weight_tables",
    )(got)


UP = [(0, 1), (1, 2), (2, 3)]
DOWN = [(1, 0), (2, 1), (3, 2)]
CORE = [(m, m ^ 1) for m in range(32)]
SAME_CORE = [[2 * q + core for q in range(16)] for core in range(2)]


def exchange(last, first):
    return lax.ppermute(last, "region", UP), lax.ppermute(first, "region", DOWN)


def among_sixteen(pieces):
    return lax.all_to_all(
        pieces, "member", split_axis=0, concat_axis=0, axis_index_groups=SAME_CORE, tiled=True
    )


def body(
    member_perts, alpha, background, obs_value, obs_weight, observed_subtile_entry, block_owner, block_count
):
    down, edge_downs, across = constants()
    send, first, last, perts_first, perts_last = place(
        block_owner[0, :, 0], block_count[0], obs_value, obs_weight, observed_subtile_entry, alpha, member_perts
    )
    top, bottom = exchange(last, first)
    term = forward(alpha, member_perts, down, across)
    got = lax.all_to_all(send, ("region", "member"), split_axis=0, concat_axis=0, tiled=True)
    mine, other = forward_edge(term, top, bottom, perts_first, perts_last, edge_downs, across)
    pieces = among_sixteen(mine + lax.ppermute(other, "member", CORE))
    w_table, v_table = tables(got)
    adjoint = adjoint_of(background, pieces, w_table, v_table)
    mine = among_sixteen(adjoint)
    adj, first, last = assemble(mine, lax.ppermute(mine, "member", CORE), perts_first, perts_last)
    top, bottom = exchange(last, first)
    grad, edge = backward(alpha, member_perts, adj.reshape(2, ROWS, COLS), down, across)
    return backward_edge(grad, edge, top, bottom, edge_downs, across)


def solution(mesh):
    placed = (
        P("member", None, "region", None),
        P("member", "region", None),
        P(None, ("region", "member"), None),
        P(("region", "member"), None, None),
        P(("region", "member"), None, None),
        P(("region", "member"), None, None),
        P(("region", "member"), None, None),
        P(("region", "member"), None),
    )
    return jax.shard_map(
        body, mesh=mesh, in_specs=placed, out_specs=P("member", "region", None), check_vma=False
    )
```

```python
import functools
import math

import jax
import jax.numpy as jnp
import ml_dtypes
import numpy as np
from jax import lax
from jax.experimental import pallas as pl
from jax.experimental.pallas import tpu as pltpu
from jax.sharding import PartitionSpec as P

HALF = 31
LENGTH_SCALE = 16.0
MEMBERS = 8
ROWS = 256
COLS = 512
EDGE = 32
SUB = 8
ENS_SCALE = 1.0 / math.sqrt(255.0)
F32 = jnp.float32
BF16 = jnp.bfloat16
PARAMS = pltpu.CompilerParams(vmem_limit_bytes=28 * 1024 * 1024)
STREAM = pltpu.CompilerParams(vmem_limit_bytes=58 * 1024 * 1024)
FORWARD = pltpu.CompilerParams(vmem_limit_bytes=52 * 1024 * 1024)
BACKWARD = pltpu.CompilerParams(vmem_limit_bytes=51 * 1024 * 1024)


def taps(offset):
    whole = np.arange(-HALF, HALF + 1).astype(np.float64)
    raw = np.exp(-whole * whole / (2.0 * LENGTH_SCALE**2))
    kernel = np.exp(-(offset.astype(np.float64) ** 2) / (2.0 * LENGTH_SCALE**2))
    return np.where(np.abs(offset) <= HALF, kernel / np.sqrt(np.sum(raw * raw)), 0.0)


def split_const(matrix):
    high = matrix.astype(ml_dtypes.bfloat16)
    low = (matrix - high.astype(np.float64)).astype(ml_dtypes.bfloat16)
    return high, low


def stack_terms(high, low, axis):
    return np.concatenate([high, high, low], axis=axis)


def band(size):
    index = np.arange(size)
    return taps(index[None, :] - index[:, None])


def constants():
    index = np.arange(EDGE)
    eye = np.eye(MEMBERS)
    top = np.kron(eye, taps(index[None, :] - EDGE - index[:, None]))
    bottom = np.kron(eye, taps(index[None, :] + EDGE - index[:, None]))
    downs = [stack_terms(*split_const(v), 1) for v in (band(ROWS), top, bottom)]
    wide = band(COLS)
    blocks = [wide[128 * i : 128 * i + 384, 256 * i : 256 * i + 256] for i in range(2)]
    across = np.stack([stack_terms(*split_const(v), 0) for v in blocks])
    return jnp.asarray(downs[0]), jnp.asarray(np.stack(downs[1:])), jnp.asarray(across)


def split(value):
    high = value.astype(BF16)
    return high, (value - high.astype(F32)).astype(BF16)


def mm(a, b):
    return jnp.dot(a, b, preferred_element_type=F32)


def terms(value, axis):
    high, low = split(value)
    return jnp.concatenate([high, low, high], axis=axis)


def down_rows(values, downs):
    return jnp.concatenate([mm(down, terms(value, 0)) for value, down in zip(values, downs)], axis=0)


def across_columns(rows, across_ref):
    high, low = split(rows)
    parts = []
    for block in range(2):
        k = slice(128 * block, 128 * block + 384)
        parts.append(mm(jnp.concatenate([high[:, k], low[:, k], high[:, k]], axis=1), across_ref[block]))
    return jnp.concatenate(parts, axis=1)


def conv(values, downs, across_ref):
    return across_columns(down_rows(values, downs), across_ref)


def whole(shape):
    return pl.BlockSpec(shape, lambda *_: (0,) * len(shape))


def cost(flops, nbytes):
    return pl.CostEstimate(flops=flops, bytes_accessed=nbytes, transcendentals=0)


VMEM = pl.BlockSpec(memory_space=pltpu.VMEM)
SMEM = pl.BlockSpec(memory_space=pltpu.SMEM)
HBM = pl.BlockSpec(memory_space=pltpu.HBM)
EDGES = (MEMBERS, EDGE, COLS)
PERTS_EDGES = (MEMBERS, 2, EDGE, COLS)
PIECES = (16, 2, SUB, COLS)


def out(shape, dtype=F32):
    return jax.ShapeDtypeStruct(shape, dtype)


def place_body(
    owner_hbm, count_hbm, value_hbm, weight_hbm, entry_hbm, alpha_hbm, perts_hbm,
    send_ref, first_ref, last_ref, perts_first_ref, perts_last_ref, owner_ref, count_ref, value_ref, weight_ref, entry_ref, used_ref, sems,
):
    pairs = [
        (owner_hbm, owner_ref), (count_hbm, count_ref),
        (value_hbm, value_ref), (weight_hbm, weight_ref), (entry_hbm, entry_ref),
        (alpha_hbm.at[:, :EDGE, :], first_ref), (alpha_hbm.at[:, ROWS - EDGE :, :], last_ref),
        (perts_hbm.at[:, :, :EDGE, :], perts_first_ref), (perts_hbm.at[:, :, ROWS - EDGE :, :], perts_last_ref),
    ]
    copies = [pltpu.make_async_copy(src, dst, sems.at[i]) for i, (src, dst) in enumerate(pairs)]
    for copy in copies:
        copy.start()
    send_ref[...] = jnp.zeros_like(send_ref)

    def clear(i, carry):
        used_ref[i] = 0
        return carry

    lax.fori_loop(0, 128, clear, 0, unroll=8)
    lane = lax.broadcasted_iota(jnp.int32, (1, 256), 1)
    for copy in copies[:5]:
        copy.wait()

    def put(b, carry):
        owner = owner_ref[b]
        slot = used_ref[owner]
        used_ref[owner] = slot + 1
        row = pl.ds(b, 1)
        weight = jnp.where(lane < count_ref[b], weight_ref[0, row, :], 0.0)
        put_at = pl.ds(slot, 1)
        send_ref[owner, put_at, 0:256] = weight
        send_ref[owner, put_at, 256:512] = weight * value_ref[0, row, :]
        send_ref[owner, put_at, 512:768] = entry_ref[0, row, :].astype(F32)
        return carry

    lax.fori_loop(0, 112, put, 0, unroll=4)
    for copy in copies[5:]:
        copy.wait()


def place(owner, count, value, weight, entry, alpha, perts):
    return pl.pallas_call(
        place_body,
        in_specs=[HBM] * 7,
        out_specs=[VMEM] * 5,
        out_shape=[
            out((128, 2, 768)), out(EDGES), out(EDGES), out(PERTS_EDGES, BF16), out(PERTS_EDGES, BF16),
        ],
        scratch_shapes=[
            pltpu.SMEM(owner.shape, jnp.int32), pltpu.SMEM(count.shape, jnp.int32),
            pltpu.VMEM(value.shape, F32), pltpu.VMEM(value.shape, F32), pltpu.VMEM(value.shape, jnp.int32),
            pltpu.SMEM((128,), jnp.int32), pltpu.SemaphoreType.DMA((9,)),
        ],
        compiler_params=STREAM,
        cost_estimate=cost(10**9, 0),
        name="place",
    )(owner, count, value, weight, entry, alpha, perts)


GROUP = 4
FIELD = (2, 16, 2, SUB, COLS)


def member_copies(source, target, sems):
    return [pltpu.make_async_copy(source.at[k], target.at[k], sems.at[k]) for k in range(MEMBERS)]


def forward_body(
    alpha_hbm, perts_hbm, down_hbm, across_hbm, term_ref,
    alpha_ref, perts_ref, down_ref, across_ref, alpha_sems, perts_sems, const_sems,
):
    alpha_copies = member_copies(alpha_hbm, alpha_ref, alpha_sems)
    perts_copies = member_copies(perts_hbm, perts_ref, perts_sems)
    down_copy = pltpu.make_async_copy(down_hbm, down_ref, const_sems.at[0])
    across_copy = pltpu.make_async_copy(across_hbm, across_ref, const_sems.at[1])
    down_copy.start()
    for base in range(0, MEMBERS, GROUP):
        for k in range(base, base + GROUP):
            alpha_copies[k].start()
        if base == 0:
            across_copy.start()
        for k in range(base, base + GROUP):
            perts_copies[k].start()
    down_copy.wait()
    rows = None
    for base in range(0, MEMBERS + GROUP, GROUP):
        before = rows
        if base < MEMBERS:
            members = range(base, base + GROUP)
            for k in members:
                alpha_copies[k].wait()
        if base == GROUP:
            across_copy.wait()
        if base > 0:
            for k in range(base - GROUP, base):
                perts_copies[k].wait()
        if base < MEMBERS:
            rows = down_rows([alpha_ref[k] for k in members], [down_ref[...]] * GROUP)
        if base > 0:
            spread = across_columns(before, across_ref)
            for field in range(2):
                total = perts_ref[base - GROUP, field].astype(F32) * spread[:ROWS]
                for m in range(1, GROUP):
                    part = spread[ROWS * m : ROWS * (m + 1)]
                    total += perts_ref[base - GROUP + m, field].astype(F32) * part
                total = total.reshape(FIELD[1:])
                if base == GROUP:
                    term_ref[field] = total
                else:
                    term_ref[field] += total


def forward(alpha, perts, down, across):
    return pl.pallas_call(
        forward_body,
        in_specs=[HBM] * 4,
        out_specs=VMEM,
        out_shape=out(FIELD),
        scratch_shapes=[
            pltpu.VMEM(alpha.shape, F32), pltpu.VMEM(perts.shape, BF16),
            pltpu.VMEM(down.shape, BF16), pltpu.VMEM(across.shape, BF16),
            pltpu.SemaphoreType.DMA((MEMBERS,)), pltpu.SemaphoreType.DMA((MEMBERS,)),
            pltpu.SemaphoreType.DMA((2,)),
        ],
        compiler_params=FORWARD,
        cost_estimate=cost(10**6, 0),
        name="forward",
    )(alpha, perts, down, across)


def forward_edge_body(
    term_ref, top_ref, bottom_ref, perts_first_ref, perts_last_ref, down_ref, across_ref, mine_ref, other_ref
):
    core = lax.rem(lax.axis_index("member"), 2)
    for field in range(2):
        mine_ref[:, field] = term_ref[field, :, core]
        other_ref[:, field] = term_ref[field, :, 1 - core]
    halo = [ref[...].reshape(MEMBERS * EDGE, COLS) for ref in (top_ref, bottom_ref)]
    spread = conv(halo, [down_ref[0], down_ref[1]], across_ref).reshape((2,) + EDGES)
    for side, p_ref in enumerate((perts_first_ref, perts_last_ref)):
        at = slice(14 * side, 14 * side + 2)
        for field in range(2):
            total = jnp.sum(p_ref[:, field].astype(F32) * spread[side], axis=0).reshape(2, 2, SUB, COLS)
            even = core == 0
            mine_ref[at, field] += jnp.where(even, total[:, 0], total[:, 1])
            other_ref[at, field] += jnp.where(even, total[:, 1], total[:, 0])


def forward_edge(term, top, bottom, perts_first, perts_last, down, across):
    return pl.pallas_call(
        forward_edge_body,
        in_specs=[VMEM] * 7,
        out_specs=[VMEM] * 2,
        out_shape=[out(PIECES), out(PIECES)],
        compiler_params=PARAMS,
        cost_estimate=cost(10**9, 6 * 2**20),
        name="forward_edge",
    )(term, top, bottom, perts_first, perts_last, down, across)


def adjoint_body(back_ref, got_ref, w_ref, v_ref, out_ref):
    state = back_ref[...] + ENS_SCALE * jnp.sum(got_ref[...], axis=0)
    out_ref[...] = jnp.broadcast_to((state * w_ref[...] - v_ref[...])[None], PIECES)


def adjoint_of(back, got, w, v):
    return pl.pallas_call(
        adjoint_body, in_specs=[VMEM] * 4, out_specs=VMEM, out_shape=out(PIECES), compiler_params=PARAMS,
        cost_estimate=cost(10**5, 2**20), name="adjoint",
    )(back, got, w, v)


def assemble_body(mine_ref, other_ref, perts_first_ref, perts_last_ref, adj_ref, first_ref, last_ref):
    core = lax.rem(lax.axis_index("member"), 2)
    for field in range(2):
        adj_ref[field, :, core] = mine_ref[:, field]
        adj_ref[field, :, 1 - core] = other_ref[:, field]
    for at, p_ref, edge_ref in ((0, perts_first_ref, first_ref), (14, perts_last_ref, last_ref)):
        rows = [adj_ref[field, at : at + 2].reshape(EDGE, COLS) for field in range(2)]
        for m in range(MEMBERS):
            edge_ref[m] = p_ref[m, 0].astype(F32) * rows[0] + p_ref[m, 1].astype(F32) * rows[1]


def assemble(mine, other, perts_first, perts_last):
    return pl.pallas_call(
        assemble_body, in_specs=[VMEM] * 4, out_specs=[VMEM] * 3,
        out_shape=[out(FIELD), out(EDGES), out(EDGES)], compiler_params=PARAMS,
        cost_estimate=cost(10**5, 2 * 2**20), name="assemble",
    )(mine, other, perts_first, perts_last)


def backward_body(
    alpha_hbm, perts_hbm, adj_ref, down_hbm, across_hbm, grad_hbm, edge_ref,
    scr, alpha_ref, perts_ref, down_ref, across_ref, alpha_sems, perts_sems, grad_sems, const_sems,
):
    alpha_copies = member_copies(alpha_hbm, alpha_ref, alpha_sems)
    perts_copies = member_copies(perts_hbm, perts_ref, perts_sems)
    copies = member_copies(scr, grad_hbm, grad_sems)
    down_copy = pltpu.make_async_copy(down_hbm, down_ref, const_sems.at[0])
    across_copy = pltpu.make_async_copy(across_hbm, across_ref, const_sems.at[1])
    down_copy.start()
    for base in range(0, MEMBERS, GROUP):
        for k in range(base, base + GROUP):
            perts_copies[k].start()
        if base == 0:
            across_copy.start()
        for k in range(base, base + GROUP):
            alpha_copies[k].start()
    down_copy.wait()
    rows = None
    for base in range(0, MEMBERS + GROUP, GROUP):
        before = rows
        if base < MEMBERS:
            for k in range(base, base + GROUP):
                perts_copies[k].wait()
        if base == GROUP:
            across_copy.wait()
        if base > 0:
            for k in range(base - GROUP, base):
                alpha_copies[k].wait()
        if base < MEMBERS:
            products = []
            for k in range(base, base + GROUP):
                product = perts_ref[k, 0].astype(F32) * adj_ref[0]
                products.append(product + perts_ref[k, 1].astype(F32) * adj_ref[1])
            rows = down_rows(products, [down_ref[...]] * GROUP)
        if base > 0:
            spread = across_columns(before, across_ref)
            for m in range(GROUP):
                k = base - GROUP + m
                scr[k] = alpha_ref[k] + ENS_SCALE * spread[ROWS * m : ROWS * (m + 1)]
                edge_ref[0, k] = scr[k, :EDGE]
                edge_ref[1, k] = scr[k, ROWS - EDGE :]
            for k in range(base - GROUP, base):
                copies[k].start()
    for copy in copies:
        copy.wait()


def backward(alpha, perts, adj, down, across):
    return pl.pallas_call(
        backward_body,
        in_specs=[HBM, HBM, VMEM, HBM, HBM],
        out_specs=[HBM, VMEM],
        out_shape=[out(alpha.shape), out((2,) + EDGES)],
        scratch_shapes=[
            pltpu.VMEM(alpha.shape, F32), pltpu.VMEM(alpha.shape, F32), pltpu.VMEM(perts.shape, BF16),
            pltpu.VMEM(down.shape, BF16), pltpu.VMEM(across.shape, BF16),
            pltpu.SemaphoreType.DMA((MEMBERS,)), pltpu.SemaphoreType.DMA((MEMBERS,)),
            pltpu.SemaphoreType.DMA((MEMBERS,)), pltpu.SemaphoreType.DMA((2,)),
        ],
        compiler_params=BACKWARD,
        cost_estimate=cost(10**6, 0),
        name="backward_own",
    )(alpha, perts, adj, down, across)


def backward_edge_body(side, grad_hbm, edge_ref, halo_ref, down_ref, across_ref, out_hbm, scr, sem):
    halo = halo_ref[...].reshape(MEMBERS * EDGE, COLS)
    spread = conv([halo], [down_ref[side]], across_ref).reshape(EDGES)
    scr[...] = edge_ref[side] + ENS_SCALE * spread
    at = (ROWS - EDGE) * side
    copy = pltpu.make_async_copy(scr, out_hbm.at[:, at : at + EDGE, :], sem)
    copy.start()
    copy.wait()


def backward_edge(side, grad, edge, halo, down, across):
    return pl.pallas_call(
        functools.partial(backward_edge_body, side),
        in_specs=[HBM] + [VMEM] * 4,
        out_specs=HBM,
        out_shape=out(grad.shape),
        input_output_aliases={0: 0},
        scratch_shapes=[pltpu.VMEM(EDGES, F32), pltpu.SemaphoreType.DMA(())],
        compiler_params=PARAMS,
        cost_estimate=cost(5 * 10**8, 3 * 2**20),
        name="backward_edge",
    )(grad, edge, halo, down, across)


SOURCES = 128
HIGH = 64
LOW = 128


def tables_body(got_ref, w_ref, v_ref, acc):
    acc[...] = jnp.zeros_like(acc)
    index = lax.broadcasted_iota(jnp.int32, (16, 512), 0).astype(F32).astype(BF16)
    one = jnp.ones((16, 512), BF16)
    zero = jnp.zeros((16, 512), BF16)

    def rows16(value):
        return jnp.broadcast_to(value, (16, 512)).astype(BF16)

    def source(s, carry):
        def line(at):
            return jnp.concatenate([got_ref[s, 0:1, at : at + 256], got_ref[s, 1:2, at : at + 256]], axis=1)

        weight, value, entry = line(0), line(256), line(512)
        chunk = jnp.floor(entry * (1.0 / LOW))
        row = jnp.floor(chunk * 0.25)
        low_at = rows16(entry - LOW * chunk) - index
        high_at = rows16(row + 16.0 * (chunk - 4.0 * row)) - index
        hits = [high_at == 16.0 * part for part in range(HIGH // 16)]
        left = []
        for quantity in (weight, value):
            first = quantity.astype(BF16).astype(F32)
            for term in (first, quantity - first):
                spread = rows16(term)
                left += [jnp.where(hit, spread, zero) for hit in hits]
        right = [jnp.where(low_at == 16.0 * part, one, zero) for part in range(LOW // 16)]
        acc[...] += lax.dot_general(
            jnp.concatenate(left, axis=0),
            jnp.concatenate(right, axis=0),
            (((1,), (1,)), ((), ())),
            preferred_element_type=F32,
        )
        return carry

    lax.fori_loop(0, SOURCES, source, 0, unroll=16)
    for ref, base in ((w_ref, 0), (v_ref, 2 * HIGH)):
        total = acc[base : base + HIGH] + acc[base + HIGH : base + 2 * HIGH]
        for field in range(2):
            for chunk in range(4):
                at = 16 * chunk + 8 * field
                ref[field, :, LOW * chunk : LOW * (chunk + 1)] = total[at : at + 8]


def tables(got):
    piece = jax.ShapeDtypeStruct((2, SUB, COLS), F32)
    return pl.pallas_call(
        tables_body,
        in_specs=[VMEM],
        out_specs=[VMEM] * 2,
        out_shape=[piece, piece],
        scratch_shapes=[pltpu.VMEM((4 * HIGH, LOW), F32)],
        compiler_params=PARAMS,
        cost_estimate=cost(12 * 10**9, 2**20),
        name="weight_tables",
    )(got)


UP = [(0, 1), (1, 2), (2, 3)]
DOWN = [(1, 0), (2, 1), (3, 2)]
CORE = [(m, m ^ 1) for m in range(32)]
SAME_CORE = [[2 * q + core for q in range(16)] for core in range(2)]


def exchange(last, first):
    return lax.ppermute(last, "region", UP), lax.ppermute(first, "region", DOWN)


def among_sixteen(pieces):
    return lax.all_to_all(
        pieces, "member", split_axis=0, concat_axis=0, axis_index_groups=SAME_CORE, tiled=True
    )


def body(
    member_perts, alpha, background, obs_value, obs_weight, observed_subtile_entry, block_owner, block_count
):
    down, edge_downs, across = constants()
    send, first, last, perts_first, perts_last = place(
        block_owner[0, :, 0], block_count[0], obs_value, obs_weight, observed_subtile_entry, alpha, member_perts
    )
    top, bottom = exchange(last, first)
    term = forward(alpha, member_perts, down, across)
    got = lax.all_to_all(send, ("region", "member"), split_axis=0, concat_axis=0, tiled=True)
    mine, other = forward_edge(term, top, bottom, perts_first, perts_last, edge_downs, across)
    pieces = among_sixteen(mine + lax.ppermute(other, "member", CORE))
    w_table, v_table = tables(got)
    adjoint = adjoint_of(background, pieces, w_table, v_table)
    mine = among_sixteen(adjoint)
    adj, first, last = assemble(mine, lax.ppermute(mine, "member", CORE), perts_first, perts_last)
    top, bottom = exchange(last, first)
    grad, edge = backward(alpha, member_perts, adj.reshape(2, ROWS, COLS), down, across)
    grad = backward_edge(0, grad, edge, top, edge_downs, across)
    return backward_edge(1, grad, edge, bottom, edge_downs, across)


def solution(mesh):
    placed = (
        P("member", None, "region", None),
        P("member", "region", None),
        P(None, ("region", "member"), None),
        P(("region", "member"), None, None),
        P(("region", "member"), None, None),
        P(("region", "member"), None, None),
        P(("region", "member"), None, None),
        P(("region", "member"), None),
    )
    return jax.shard_map(
        body, mesh=mesh, in_specs=placed, out_specs=P("member", "region", None), check_vma=False
    )
```
